32 devices in a mesh: seq: 16 (over z, y, core), tp: 2 (over x).
Axes of the slice: x: 2, y: 2, z: 4, core: 2. Of those that a mesh axis runs over, the one named last changes fastest.
Arguments:
- queries: bfloat16 [4096, 8, 8, 128], P('seq', None, 'tp'), may hold values from -6 to 6
- keys: bfloat16 [4096, 8, 128], P('seq'), may hold values from -6 to 6
- values: bfloat16 [4096, 8, 128], P('seq'), may hold values from -6 to 6
- grad_out: bfloat16 [4096, 8, 8, 128], P('seq', None, 'tp'), may hold values from -6 to 6
- exponents: int32 [32, 8, 8], P('seq', None, 'tp'), may hold values from -2 to 2
- lengths: int32 [32], replicated, may hold values from 1 to 256, 4096 in all
Outputs:
- grad_queries: bfloat16 [4096, 8, 8, 128], P('seq', None, 'tp')
- grad_keys: bfloat16 [4096, 8, 128], P('seq', 'tp')
- grad_values: bfloat16 [4096, 8, 128], P('seq', 'tp')
The draws below stay inside these ranges and needn't reach their ends.
Inputs may be any that keep to these rules, and one draw needn't show every extreme that they name: No document has more than 256 tokens (at least one has exactly 256); the lengths sum to 4096. `exponents`: one exponent for each block of 128 tokens of one query head.
All inputs are finite; a program needn't handle non-finite values.
Results may differ from the reference program's by a relative error of at most 0.03.
Values may be sent and summed in bfloat16 or wider, within the bound.
A program may use at most 64 MiB of HBM per device.

```python
import math
import jax
import jax.numpy as jnp
import numpy as np
from jax import lax

G = 8
HD = 128
R = 8
TOK_DEV = 256
EB = 128
TOKENS = 4096
DOCS = 32


def draw_queries(key, part):
    key = jax.random.fold_in(key, 11)
    result = jnp.clip(jax.random.normal(key, (TOKENS, G, R, HD), jnp.float32), -6.0, 6.0)
    return result.astype(jnp.bfloat16)


def draw_keys(key, part):
    key = jax.random.fold_in(key, 12)
    result = jnp.clip(jax.random.normal(key, (TOKENS, G, HD), jnp.float32), -6.0, 6.0)
    return result.astype(jnp.bfloat16)


def plant(values, stream_key, low, high):
    longest = values.shape.index(max(values.shape))
    spots = []
    for shift in (0, 1):
        where = [jax.random.randint(jax.random.fold_in(stream_key, axis), (), 0, length) for axis, length in enumerate(values.shape)]
        where[longest] = (where[longest] + shift) % values.shape[longest]
        spots.append(tuple(where))
    return values.at[spots[0]].set(low).at[spots[1]].set(high)


def block_levels(stream_key, extent, cuts, smallest, top_value):
    loudness, own = 1.0, jax.random.fold_in(stream_key, 6)
    for dim, shards_of in cuts:
        steps = jnp.exp(jax.random.uniform(jax.random.fold_in(own, dim), (shards_of,), jnp.float32, smallest / len(cuts), top_value / len(cuts)))
        loudness = loudness * jnp.repeat(steps, extent[dim] // shards_of).reshape([-1 if axis == dim else 1 for axis in range(len(extent))])
    return loudness


def split_up(number_of, total, bound, skew):
    weights = [(1 << 20) // math.isqrt(standing ** skew) + 1 for standing in range(2, number_of + 1)]
    rest, counts = total - bound - (number_of - 1), [1] * (number_of - 1)
    while rest > 0:
        movable = [i for i in range(number_of - 1) if counts[i] < bound]
        mass, budget = sum([weights[i] for i in movable]), rest
        for i in movable:
            more = min(bound - counts[i], max(1, budget * weights[i] // mass), rest)
            counts[i] = counts[i] + more
            rest = rest - more
    return np.array([bound] + counts)


def ragged_sizes(own_key, amount, total, limit, lean):
    if amount == 2:
        one = jax.random.randint(own_key, (), max(1, total - limit), min(limit, total - 1) + 1)
        return jnp.stack([one, total - one])
    sizes = jnp.asarray(split_up(amount, total, limit, lean), jnp.int32)
    twos = (amount - 1) // 2
    source_of, receiver = sizes[1:1 + 2 * twos:2], sizes[2:2 + 2 * twos:2]
    margin = jnp.minimum(source_of - 1, limit - receiver)
    moved = jax.random.randint(jax.random.fold_in(own_key, 1), (twos,), 0, 1 << 20) % (margin + 1)
    sizes = sizes.at[1:1 + 2 * twos:2].set(source_of - moved).at[2:2 + 2 * twos:2].set(receiver + moved)
    return sizes[jax.random.permutation(jax.random.fold_in(own_key, 2), amount)]


def normal_values(rng, shape, width, most, pieces=(), kind=jnp.bfloat16):
    array = width * jax.random.normal(rng, shape, jnp.float32)
    if pieces:
        array = array * block_levels(rng, shape, pieces, -0.22, 0.18)
    return jnp.clip(array, -most, most).astype(kind)


def setup_inputs(seed: int = 0) -> dict:
    streams_of = jax.random.split(jax.random.key(seed), 7)
    queries = draw_queries(jax.random.fold_in(streams_of[6], 71), 0)
    keys = draw_keys(jax.random.fold_in(streams_of[6], 71), 0)
    values = normal_values(streams_of[2], (TOKENS, G, HD), 1.0, 6.0, ((0, 16),))
    grad_out = normal_values(streams_of[3], (TOKENS, G, R, HD), 1.0, 6.0, ((0, 16), (2, 2)))
    exponents = plant(jax.random.randint(streams_of[4], (TOKENS // EB, G, R), -2, 3), jax.random.fold_in(streams_of[4], 1), -2, 2).astype(jnp.int32)
    lengths = ragged_sizes(streams_of[5], DOCS, TOKENS, TOK_DEV, 1).astype(jnp.int32)
    return {"queries": queries, "keys": keys, "values": values, "grad_out": grad_out, "exponents": exponents, "lengths": lengths}


def doc_numbers(lengths, positions):
    doc_ends = jnp.cumsum(lengths).astype(jnp.int32)
    return jnp.sum((doc_ends[None, :] <= positions[:, None]).astype(jnp.int32), axis=1)


def block_grads(query_blk, dout_blk, key_window, value_window, allowed, scaling):
    query_f = query_blk.astype(jnp.float32)
    dout_f = dout_blk.astype(jnp.float32)
    key_f = key_window.astype(jnp.float32)
    value_f = value_window.astype(jnp.float32)
    scores = jnp.einsum('qgrd,kgd->grqk', query_f, key_f) * scaling
    scores = jnp.where(allowed[None, None], scores, -1e30)
    row_max = jnp.max(scores, axis=-1, keepdims=True)
    shifted = jnp.exp(scores - row_max)
    row_sum = jnp.sum(shifted, axis=-1, keepdims=True)
    attn_w = shifted / row_sum
    attn_low = lax.optimization_barrier(attn_w.astype(jnp.bfloat16)).astype(jnp.float32)
    attn_out = jnp.einsum('grqk,kgd->qgrd', attn_low, value_f).astype(jnp.bfloat16)
    attn_out = lax.optimization_barrier(attn_out).astype(jnp.float32)
    row_delta = jnp.transpose(jnp.sum(dout_f * attn_out, axis=-1), (1, 2, 0))[..., None]
    grad_probs = jnp.einsum('qgrd,kgd->grqk', dout_f, value_f)
    grad_scores = (scaling * attn_w * (grad_probs - row_delta)).astype(jnp.bfloat16)
    grad_scores = lax.optimization_barrier(grad_scores).astype(jnp.float32)
    grad_query = jnp.einsum('grqk,kgd->qgrd', grad_scores, key_f).astype(jnp.bfloat16)
    grad_key = jnp.einsum('grqk,qgrd->kgd', grad_scores, query_f)
    grad_value = jnp.einsum('grqk,qgrd->kgd', attn_low, dout_f)
    return grad_query, grad_key, grad_value


def reference(queries, keys, values, grad_out, exponents, lengths):
    token_count = queries.shape[0]
    block_count = token_count // TOK_DEV
    scaling = HD ** -0.5
    factor = jnp.exp2(exponents.astype(jnp.float32))
    scaled = grad_out.reshape(token_count // EB, EB, G, R, HD).astype(jnp.float32) * factor[:, None, :, :, None]
    scaled = scaled.astype(jnp.bfloat16).reshape(token_count, G, R, HD)
    padding = jnp.zeros((TOK_DEV, G, HD), keys.dtype)
    key_padded = jnp.concatenate([padding, keys], axis=0)
    value_padded = jnp.concatenate([padding, values], axis=0)

    def one_block(block_index):
        start = (block_index * TOK_DEV).astype(jnp.int32)
        query_blk = lax.dynamic_slice_in_dim(queries, start, TOK_DEV, 0)
        dout_blk = lax.dynamic_slice_in_dim(scaled, start, TOK_DEV, 0)
        key_window = lax.dynamic_slice_in_dim(key_padded, start, 2 * TOK_DEV, 0)
        value_window = lax.dynamic_slice_in_dim(value_padded, start, 2 * TOK_DEV, 0)
        query_pos = start + jnp.arange(TOK_DEV, dtype=jnp.int32)
        key_pos = start - TOK_DEV + jnp.arange(2 * TOK_DEV, dtype=jnp.int32)
        query_doc = doc_numbers(lengths, query_pos)
        key_doc = doc_numbers(lengths, key_pos)
        allowed = (query_doc[:, None] == key_doc[None, :]) & (key_pos[None, :] <= query_pos[:, None]) & (key_pos[None, :] >= 0)
        return block_grads(query_blk, dout_blk, key_window, value_window, allowed, scaling)

    grad_query, key_terms, value_terms = lax.map(one_block, jnp.arange(block_count, dtype=jnp.int32))
    tail = jnp.zeros((1, TOK_DEV, G, HD), key_terms.dtype)
    grad_keys = key_terms[:, TOK_DEV:] + jnp.concatenate([key_terms[1:, :TOK_DEV], tail], axis=0)
    grad_values = value_terms[:, TOK_DEV:] + jnp.concatenate([value_terms[1:, :TOK_DEV], tail], axis=0)
    grad_queries = grad_query.reshape(token_count, G, R, HD)
    return (grad_queries,
            grad_keys.astype(jnp.bfloat16).reshape(token_count, G, HD),
            grad_values.astype(jnp.bfloat16).reshape(token_count, G, HD))
```

```python
import functools
import math
import jax
import jax.numpy as jnp
from jax import lax
from jax.experimental import pallas as pl
from jax.experimental.pallas import tpu as pltpu
from jax.sharding import PartitionSpec as P

F32 = jnp.float32
BF16 = jnp.bfloat16
NT = (((1,), (1,)), ((), ()))
TN = (((0,), (0,)), ((), ()))


def passed_along(block, axis, distance):
    devices = range(lax.axis_size(axis))
    route = [(i - distance, i) for i in devices if i - distance in devices]
    return lax.ppermute(block, axis, route)


def fill_bias(bias, lengths, first, heads, chunk):
    chunks, keys, rows = bias.shape
    for j in range(chunks):
        query_pos = first + chunk * j + lax.broadcasted_iota(jnp.int32, (1, rows), 1) // heads

        def step(d, carry):
            end, start = carry
            end = end + lengths[d]
            return end, jnp.where(query_pos >= end, end, start)

        _, start = lax.fori_loop(
            0, lengths.shape[0], step, (jnp.int32(0), jnp.zeros((1, rows), jnp.int32))
        )
        key_pos = first + chunk * (j + 1) - keys + lax.broadcasted_iota(jnp.int32, (keys, rows), 0)
        allowed = (key_pos >= start) & (key_pos <= query_pos)
        bias[j] = jnp.where(allowed, 0.0, -1e30).astype(F32)


def row_factor(exponents, block, group, heads, rows):
    head = lax.broadcasted_iota(jnp.int32, (1, rows), 1) % heads
    level = jnp.full((1, rows), exponents[block, group, 0], jnp.int32)
    for r in range(1, heads):
        level = jnp.where(head == r, exponents[block, group, r], level)
    factor = jnp.full((1, rows), 1.0, F32)
    for value in (-2, -1, 1, 2):
        factor = jnp.where(level == value, 2.0**value, factor)
    return factor


def group_terms(query, grad, key_ref, value_ref, bias, factors, grad_key, grad_value):
    chunks, keys, rows = bias.shape
    chunk = (key_ref.shape[0] - keys) // (chunks - 1)
    scaling = query.shape[1] ** -0.5
    grad_key[...] = jnp.zeros_like(grad_key)
    grad_value[...] = jnp.zeros_like(grad_value)
    grad_query = []
    for j in range(chunks):
        window = pl.ds(chunk * j, keys)
        q = query[rows * j : rows * (j + 1)]
        g = grad[rows * j : rows * (j + 1)]
        k = key_ref[window]
        v = value_ref[window]
        scores = lax.dot_general(k, q, NT, preferred_element_type=F32) + bias[j]
        top = jnp.max(scores, axis=0, keepdims=True)
        e = jnp.exp2((scores - top) * (scaling * math.log2(math.e)))
        inverse = 1.0 / jnp.sum(e, axis=0, keepdims=True)
        grad_probs = lax.dot_general(v, g, NT, preferred_element_type=F32)
        delta = jnp.sum(e * grad_probs, axis=0, keepdims=True) * inverse
        p = e * (inverse * factors[j] * scaling)
        low = p.astype(BF16)
        ds = (p * (grad_probs - delta)).astype(BF16)
        grad_query.append(lax.dot_general(ds, k, TN, preferred_element_type=F32).astype(BF16))
        grad_key[window] += jnp.dot(ds, q, preferred_element_type=F32)
        grad_value[window] += jnp.dot(low, g, preferred_element_type=F32)
    return jnp.concatenate(grad_query, axis=0)


def local_kernel(
    chunk, lengths, exponents, q_ref, go_ref, pk_ref, pv_ref, k_ref, v_ref,
    gq_ref, own_k, own_v, back_k, back_v, wide, key_win, value_win, bias, acc_k, acc_v,
):
    group = pl.program_id(0)
    tokens, groups, width = k_ref.shape
    heads = q_ref.shape[2]
    first = lax.axis_index("seq") * tokens

    @pl.when(group == 0)
    def _():
        fill_bias(bias, lengths, first, heads, chunk)
        for src, dst, at in (
            (pk_ref, key_win, 0), (k_ref, key_win, tokens),
            (pv_ref, value_win, 0), (v_ref, value_win, tokens),
        ):
            wide[...] = src[...].astype(F32).reshape(tokens * groups, width)
            for i in range(groups):
                dst[i, pl.ds(at, tokens)] = wide[pl.ds(i, tokens, stride=groups)].astype(BF16)

    chunks, _, rows = bias.shape
    blocks = exponents.shape[0]
    factors = [
        row_factor(exponents, (j * blocks) // chunks, group, heads, rows) for j in range(chunks)
    ]
    out = group_terms(
        q_ref[...].reshape(tokens * heads, width), go_ref[...].reshape(tokens * heads, width),
        key_win.at[group], value_win.at[group], bias, factors, acc_k, acc_v,
    )
    gq_ref[...] = out.reshape(tokens, 1, heads, width)
    back_k[...] = acc_k[:tokens].astype(BF16)
    own_k[...] = acc_k[tokens:]
    back_v[...] = (acc_v[:tokens] * width**0.5).astype(BF16)
    own_v[...] = acc_v[tokens:] * width**0.5


def per_device(queries, keys, values, grad_out, exponents, lengths):
    tokens, groups, heads, width = queries.shape
    chunks = 4
    chunk = tokens // chunks
    window = tokens + chunk
    pk, pv = passed_along((keys, values), "seq", 1)
    smem = pl.BlockSpec(memory_space=pltpu.SMEM)
    vmem = pl.BlockSpec(memory_space=pltpu.VMEM)
    rows_spec = pl.BlockSpec((tokens, 1, heads, width), lambda g: (0, g, 0, 0))
    term_spec = pl.BlockSpec((None, tokens, width), lambda g: (g, 0, 0))
    gq, own_k, own_v, back_k, back_v = pl.pallas_call(
        functools.partial(local_kernel, chunk),
        grid=(groups,),
        in_specs=[smem, smem, rows_spec, rows_spec, vmem, vmem, vmem, vmem],
        out_specs=[rows_spec, term_spec, term_spec, term_spec, term_spec],
        out_shape=[
            jax.ShapeDtypeStruct(queries.shape, BF16),
            jax.ShapeDtypeStruct((groups, tokens, width), F32),
            jax.ShapeDtypeStruct((groups, tokens, width), F32),
            jax.ShapeDtypeStruct((groups, tokens, width), BF16),
            jax.ShapeDtypeStruct((groups, tokens, width), BF16),
        ],
        scratch_shapes=[
            pltpu.VMEM((tokens * groups, width), F32),
            pltpu.VMEM((groups, 2 * tokens, width), BF16),
            pltpu.VMEM((groups, 2 * tokens, width), BF16),
            pltpu.VMEM((chunks, window, chunk * heads), F32),
            pltpu.VMEM((2 * tokens, width), F32),
            pltpu.VMEM((2 * tokens, width), F32),
        ],
        compiler_params=pltpu.CompilerParams(vmem_limit_bytes=48 * 1024 * 1024),
    )(lengths, exponents, queries, grad_out, pk, pv, keys, values)
    key_total = own_k + passed_along(back_k, "seq", -1).astype(F32)
    value_total = own_v + passed_along(back_v, "seq", -1).astype(F32)
    summed_keys, summed_values = (
        lax.psum_scatter(key_total, "tp", scatter_dimension=0, tiled=True),
        lax.psum_scatter(value_total, "tp", scatter_dimension=0, tiled=True),
    )
    return (
        gq,
        jnp.moveaxis(summed_keys, 0, 1).astype(BF16),
        jnp.moveaxis(summed_values, 0, 1).astype(BF16),
    )


def solution(mesh):
    placed = (
        P("seq", None, "tp", None),
        P("seq", None, None),
        P("seq", None, None),
        P("seq", None, "tp", None),
        P("seq", None, "tp"),
        P(),
    )
    return jax.shard_map(
        per_device,
        mesh=mesh,
        in_specs=placed,
        out_specs=(P("seq", None, "tp", None), P("seq", "tp", None), P("seq", "tp", None)),
        check_vma=False,
    )
```

```python
import functools
import math
import jax
import jax.numpy as jnp
from jax import lax
from jax.experimental import pallas as pl
from jax.experimental.pallas import tpu as pltpu
from jax.sharding import PartitionSpec as P

F32 = jnp.float32
BF16 = jnp.bfloat16
NT = (((1,), (1,)), ((), ()))
TN = (((0,), (0,)), ((), ()))
MESH = pl.DeviceIdType.MESH
LAG = 1


def fill_bias(bias, lengths, first, heads, chunk):
    chunks, keys, rows = bias.shape
    for j in range(chunks):
        query_pos = first + chunk * j + lax.broadcasted_iota(jnp.int32, (1, rows), 1) // heads

        def step(d, carry):
            end, start = carry
            end = end + lengths[d]
            return end, jnp.where(query_pos >= end, end, start)

        _, start = lax.fori_loop(
            0, lengths.shape[0], step, (jnp.int32(0), jnp.zeros((1, rows), jnp.int32))
        )
        key_pos = first + chunk * (j + 1) - keys + lax.broadcasted_iota(jnp.int32, (keys, rows), 0)
        allowed = (key_pos >= start) & (key_pos <= query_pos)
        bias[j] = jnp.where(allowed, 0.0, -1e30).astype(F32)


def row_factor(exponents, block, group, heads, rows):
    head = lax.broadcasted_iota(jnp.int32, (1, rows), 1) % heads
    level = jnp.full((1, rows), exponents[block, 0, group], jnp.int32)
    for r in range(1, heads):
        level = jnp.where(head == r, exponents[block, r, group], level)
    factor = jnp.full((1, rows), 1.0, F32)
    for value in (-2, -1, 1, 2):
        factor = jnp.where(level == value, 2.0**value, factor)
    return factor


def group_terms(query, grad, key_ref, value_ref, bias, factors, grad_key, grad_value):
    chunks, keys, rows = bias.shape
    chunk = (key_ref.shape[0] - keys) // (chunks - 1)
    scaling = query.shape[1] ** -0.5
    grad_key[...] = jnp.zeros_like(grad_key)
    grad_value[...] = jnp.zeros_like(grad_value)
    grad_query = []
    for j in range(chunks):
        window = pl.ds(chunk * j, keys)
        q = query[rows * j : rows * (j + 1)]
        g = grad[rows * j : rows * (j + 1)]
        k = key_ref[window]
        v = value_ref[window]
        scores = lax.dot_general(k, q, NT, preferred_element_type=F32) + bias[j]
        top = jnp.max(scores, axis=0, keepdims=True)
        e = jnp.exp2((scores - top) * (scaling * math.log2(math.e)))
        inverse = 1.0 / jnp.sum(e, axis=0, keepdims=True)
        grad_probs = lax.dot_general(v, g, NT, preferred_element_type=F32)
        delta = jnp.sum(e * grad_probs, axis=0, keepdims=True) * inverse
        p = e * (inverse * factors[j] * scaling)
        low = p.astype(BF16)
        ds = (p * (grad_probs - delta)).astype(BF16)
        grad_query.append(lax.dot_general(ds, k, TN, preferred_element_type=F32).astype(BF16))
        grad_key[window] += jnp.dot(ds, q, preferred_element_type=F32)
        grad_value[window] += jnp.dot(low, g, preferred_element_type=F32)
    return jnp.concatenate(grad_query, axis=0)


def group_at(i, rank, ranks, share):
    return lax.rem(rank + 1 + i // share, ranks) * share + lax.rem(i, share)


def fused_kernel(
    chunk, shards, ranks,
    lengths, exponents, q_ref, go_ref, k_ref, v_ref,
    gq_ref, gk_ref, gv_ref,
    wide_k, wide_v, own_k, own_v, prev_k, prev_v, window_k, window_v, bias,
    acc_k, acc_v, own, back_out, back_in, cross_out, cross_in, out_k, out_v,
    win_send, win_recv, back_send, back_recv, cross_send, cross_recv,
):
    tokens, groups, width = k_ref.shape
    heads = q_ref.shape[2]
    share = groups // ranks
    foreign = groups - share
    shard, rank = lax.axis_index("seq"), lax.axis_index("tp")
    has_next, has_prev = shard < shards - 1, shard > 0
    unscale = width**0.5
    i = pl.program_id(0)
    group = group_at(i, rank, ranks, share)

    def window_copies(i):
        return [
            pltpu.make_async_remote_copy(
                src_ref=src.at[i], dst_ref=dst.at[i],
                send_sem=win_send.at[part, i], recv_sem=win_recv.at[part, i],
                device_id=(shard + 1, rank), device_id_type=MESH,
            )
            for part, (src, dst) in enumerate(((own_k, prev_k), (own_v, prev_v)))
        ]

    def back_copy(i):
        return pltpu.make_async_remote_copy(
            src_ref=back_out.at[i], dst_ref=back_in.at[i],
            send_sem=back_send.at[i], recv_sem=back_recv.at[i],
            device_id=(shard - 1, rank), device_id_type=MESH,
        )

    def cross_copy(i):
        return pltpu.make_async_remote_copy(
            src_ref=cross_out.at[i], dst_ref=cross_in.at[i],
            send_sem=cross_send.at[i], recv_sem=cross_recv.at[i],
            device_id=(shard, lax.rem(rank + 1 + i // share, ranks)), device_id_type=MESH,
        )

    @pl.when(i == 0)
    def _():
        barrier = pltpu.get_barrier_semaphore()

        @pl.when(has_next)
        def _():
            pl.semaphore_signal(barrier, inc=1, device_id=(shard + 1, rank), device_id_type=MESH)

        @pl.when(has_prev)
        def _():
            pl.semaphore_signal(barrier, inc=1, device_id=(shard - 1, rank), device_id_type=MESH)

        for other in range(1, ranks):
            peer = lax.rem(rank + other, ranks)
            pl.semaphore_signal(barrier, inc=1, device_id=(shard, peer), device_id_type=MESH)
        wide_k[...] = k_ref[...].astype(F32).reshape(tokens * groups, width)
        wide_v[...] = v_ref[...].astype(F32).reshape(tokens * groups, width)
        for n in range(groups):
            rows = pl.ds(group_at(n, rank, ranks, share), tokens, stride=groups)
            own_k[n] = wide_k[rows].astype(BF16)
            own_v[n] = wide_v[rows].astype(BF16)
        pl.semaphore_wait(
            barrier, ranks - 1 + has_next.astype(jnp.int32) + has_prev.astype(jnp.int32)
        )

        @pl.when(has_next)
        def _():
            for n in range(groups):
                for copy in window_copies(n):
                    copy.start()

        fill_bias(bias, lengths, shard * tokens, heads, chunk)

    chunks, _, rows = bias.shape
    blocks = exponents.shape[0]

    def add_back(i):
        @pl.when(has_next)
        def _():
            back_copy(i).wait_recv()
            own[i] += back_in[i].astype(F32)

    def pass_on(i):
        add_back(i)
        cross_out[i] = own[i].astype(BF16)
        cross_copy(i).start()

    def finish(i):
        add_back(i)
        local = i - foreign
        total = own[i]
        for other in range(ranks - 1):
            cross_copy(other * share + local).wait_recv()
            total = total + cross_in[other * share + local].astype(F32)
        out_k[pl.ds(local, tokens, stride=share)] = total[0]
        out_v[pl.ds(local, tokens, stride=share)] = total[1]

    @pl.when(has_prev)
    def _():
        for copy in window_copies(i):
            copy.wait_recv()
        window_k[:tokens] = prev_k[i]
        window_v[:tokens] = prev_v[i]

    @pl.when(jnp.logical_not(has_prev))
    def _():
        window_k[:tokens] = jnp.zeros((tokens, width), BF16)
        window_v[:tokens] = jnp.zeros((tokens, width), BF16)

    window_k[tokens:] = own_k[i]
    window_v[tokens:] = own_v[i]
    factors = [
        row_factor(exponents, (j * blocks) // chunks, group, heads, rows) for j in range(chunks)
    ]
    out = group_terms(
        q_ref[...].reshape(tokens * heads, width), go_ref[...].reshape(tokens * heads, width),
        window_k, window_v, bias, factors, acc_k, acc_v,
    )
    gq_ref[...] = out.reshape(tokens, 1, heads, width)
    own[i, 0] = acc_k[tokens:]
    own[i, 1] = acc_v[tokens:] * unscale

    @pl.when(has_prev)
    def _():
        back_out[i, 0] = acc_k[:tokens].astype(BF16)
        back_out[i, 1] = (acc_v[:tokens] * unscale).astype(BF16)
        back_copy(i).start()

    @pl.when(jnp.logical_and(i >= LAG, i < foreign + LAG))
    def _():
        pass_on(i - LAG)

    @pl.when(i >= foreign + LAG)
    def _():
        finish(i - LAG)

    @pl.when(i == groups - 1)
    def _():
        for n in range(groups - LAG, groups):
            finish(n)
        gk_ref[...] = out_k[...].astype(BF16).reshape(tokens, share, width)
        gv_ref[...] = out_v[...].astype(BF16).reshape(tokens, share, width)

        @pl.when(has_next)
        def _():
            for n in range(groups):
                for copy in window_copies(n):
                    copy.wait_send()

        @pl.when(has_prev)
        def _():
            for n in range(groups):
                back_copy(n).wait_send()

        for n in range(foreign):
            cross_copy(n).wait_send()


def per_device(shards, ranks, queries, keys, values, grad_out, exponents, lengths):
    tokens, groups, heads, width = queries.shape
    chunks = 4
    chunk = tokens // chunks
    share = groups // ranks
    foreign = groups - share
    levels = jnp.swapaxes(exponents, 1, 2)
    smem = pl.BlockSpec(memory_space=pltpu.SMEM)
    vmem = pl.BlockSpec(memory_space=pltpu.VMEM)
    rows_spec = pl.BlockSpec(
        (tokens, 1, heads, width),
        lambda i: (0, group_at(i, lax.axis_index("tp"), ranks, share), 0, 0),
    )
    pair = (2, tokens, width)
    dma = pltpu.SemaphoreType.DMA
    return pl.pallas_call(
        functools.partial(fused_kernel, chunk, shards, ranks),
        grid=(groups,),
        in_specs=[smem, smem, rows_spec, rows_spec, vmem, vmem],
        out_specs=[rows_spec, vmem, vmem],
        out_shape=[
            jax.ShapeDtypeStruct(queries.shape, BF16),
            jax.ShapeDtypeStruct((tokens, share, width), BF16),
            jax.ShapeDtypeStruct((tokens, share, width), BF16),
        ],
        scratch_shapes=[
            pltpu.VMEM((tokens * groups, width), F32),
            pltpu.VMEM((tokens * groups, width), F32),
            pltpu.VMEM((groups, tokens, width), BF16),
            pltpu.VMEM((groups, tokens, width), BF16),
            pltpu.VMEM((groups, tokens, width), BF16),
            pltpu.VMEM((groups, tokens, width), BF16),
            pltpu.VMEM((2 * tokens, width), BF16),
            pltpu.VMEM((2 * tokens, width), BF16),
            pltpu.VMEM((chunks, tokens + chunk, chunk * heads), F32),
            pltpu.VMEM((2 * tokens, width), F32),
            pltpu.VMEM((2 * tokens, width), F32),
            pltpu.VMEM((groups,) + pair, F32),
            pltpu.VMEM((groups,) + pair, BF16),
            pltpu.VMEM((groups,) + pair, BF16),
            pltpu.VMEM((foreign,) + pair, BF16),
            pltpu.VMEM((foreign,) + pair, BF16),
            pltpu.VMEM((tokens * share, width), F32),
            pltpu.VMEM((tokens * share, width), F32),
            dma((2, groups)), dma((2, groups)), dma((groups,)), dma((groups,)),
            dma((foreign,)), dma((foreign,)),
        ],
        compiler_params=pltpu.CompilerParams(
            collective_id=0, has_side_effects=True, vmem_limit_bytes=60 * 1024 * 1024
        ),
    )(lengths, levels, queries, grad_out, keys, values)


def solution(mesh):
    placed = (
        P("seq", None, "tp", None),
        P("seq", None, None),
        P("seq", None, None),
        P("seq", None, "tp", None),
        P("seq", None, "tp"),
        P(),
    )
    return jax.shard_map(
        functools.partial(per_device, mesh.shape["seq"], mesh.shape["tp"]),
        mesh=mesh,
        in_specs=placed,
        out_specs=(P("seq", None, "tp", None), P("seq", "tp", None), P("seq", "tp", None)),
        check_vma=False,
    )
```

```python
import functools
import math
import jax
import jax.numpy as jnp
from jax import lax
from jax.experimental import pallas as pl
from jax.experimental.pallas import tpu as pltpu
from jax.sharding import PartitionSpec as P

F32 = jnp.float32
BF16 = jnp.bfloat16
NT = (((1,), (1,)), ((), ()))
TN = (((0,), (0,)), ((), ()))
MESH = pl.DeviceIdType.MESH
AHEAD = 3
LAG = 2


def fill_bias(bias, lengths, first, heads, chunk):
    chunks, keys, rows = bias.shape
    for j in range(chunks):
        query_pos = first + chunk * j + lax.broadcasted_iota(jnp.int32, (1, rows), 1) // heads

        def step(d, carry):
            end, start = carry
            end = end + lengths[d]
            return end, jnp.where(query_pos >= end, end, start)

        _, start = lax.fori_loop(
            0, lengths.shape[0], step, (jnp.int32(0), jnp.zeros((1, rows), jnp.int32))
        )
        key_pos = first + chunk * (j + 1) - keys + lax.broadcasted_iota(jnp.int32, (keys, rows), 0)
        allowed = (key_pos >= start) & (key_pos <= query_pos)
        bias[j] = jnp.where(allowed, 0.0, -1e30).astype(F32)


def row_factor(exponents, block, group, heads, rows):
    head = lax.broadcasted_iota(jnp.int32, (1, rows), 1) % heads
    level = jnp.full((1, rows), exponents[block, 0, group], jnp.int32)
    for r in range(1, heads):
        level = jnp.where(head == r, exponents[block, r, group], level)
    factor = jnp.full((1, rows), 1.0, F32)
    for value in (-2, -1, 1, 2):
        factor = jnp.where(level == value, 2.0**value, factor)
    return factor


def group_terms(query, grad, key_ref, value_ref, bias, factors, grad_key, grad_value):
    chunks, keys, rows = bias.shape
    chunk = (key_ref.shape[0] - keys) // (chunks - 1)
    scaling = query.shape[1] ** -0.5
    grad_key[...] = jnp.zeros_like(grad_key)
    grad_value[...] = jnp.zeros_like(grad_value)
    grad_query = []
    for j in range(chunks):
        window = pl.ds(chunk * j, keys)
        q = query[rows * j : rows * (j + 1)]
        g = grad[rows * j : rows * (j + 1)]
        k = key_ref[window]
        v = value_ref[window]
        scores = lax.dot_general(k, q, NT, preferred_element_type=F32) + bias[j]
        top = jnp.max(scores, axis=0, keepdims=True)
        e = jnp.exp2((scores - top) * (scaling * math.log2(math.e)))
        inverse = 1.0 / jnp.sum(e, axis=0, keepdims=True)
        grad_probs = lax.dot_general(v, g, NT, preferred_element_type=F32)
        delta = jnp.sum(e * grad_probs, axis=0, keepdims=True) * inverse
        p = e * (inverse * factors[j] * scaling)
        low = p.astype(BF16)
        ds = (p * (grad_probs - delta)).astype(BF16)
        grad_query.append(lax.dot_general(ds, k, TN, preferred_element_type=F32).astype(BF16))
        grad_key[window] += jnp.dot(ds, q, preferred_element_type=F32)
        grad_value[window] += jnp.dot(low, g, preferred_element_type=F32)
    return jnp.concatenate(grad_query, axis=0)


def group_at(i, rank, ranks, share):
    return lax.rem(rank + 1 + i // share, ranks) * share + lax.rem(i, share)


def fused_kernel(
    chunk, shards, ranks,
    lengths, exponents, q_ref, go_ref, k_ref, v_ref,
    gq_ref, gk_ref, gv_ref,
    wide_k, wide_v, own_k, own_v, prev_k, prev_v, window_k, window_v, bias,
    acc_k, acc_v, own, back_out, back_in, cross_out, cross_in, out_k, out_v,
    win_send, win_recv, back_send, back_recv, cross_send, cross_recv,
):
    tokens, groups, width = k_ref.shape
    heads = q_ref.shape[2]
    share = groups // ranks
    foreign = groups - share
    shard, rank = lax.axis_index("seq"), lax.axis_index("tp")
    has_next, has_prev = shard < shards - 1, shard > 0
    unscale = width**0.5
    i = pl.program_id(0)
    group = group_at(i, rank, ranks, share)

    def window_copies(i):
        return [
            pltpu.make_async_remote_copy(
                src_ref=src.at[i], dst_ref=dst.at[i],
                send_sem=win_send.at[part, i], recv_sem=win_recv.at[part, i],
                device_id=(shard + 1, rank), device_id_type=MESH,
            )
            for part, (src, dst) in enumerate(((own_k, prev_k), (own_v, prev_v)))
        ]

    def send_window(i):
        @pl.when(has_next)
        def _():
            for copy in window_copies(i):
                copy.start()

    def back_copy(i):
        return pltpu.make_async_remote_copy(
            src_ref=back_out.at[i], dst_ref=back_in.at[i],
            send_sem=back_send.at[i], recv_sem=back_recv.at[i],
            device_id=(shard - 1, rank), device_id_type=MESH,
        )

    def cross_copy(i):
        return pltpu.make_async_remote_copy(
            src_ref=cross_out.at[i], dst_ref=cross_in.at[i],
            send_sem=cross_send.at[i], recv_sem=cross_recv.at[i],
            device_id=(shard, lax.rem(rank + 1 + i // share, ranks)), device_id_type=MESH,
        )

    @pl.when(i == 0)
    def _():
        barrier = pltpu.get_barrier_semaphore()

        @pl.when(has_next)
        def _():
            pl.semaphore_signal(barrier, inc=1, device_id=(shard + 1, rank), device_id_type=MESH)

        @pl.when(has_prev)
        def _():
            pl.semaphore_signal(barrier, inc=1, device_id=(shard - 1, rank), device_id_type=MESH)

        for other in range(1, ranks):
            peer = lax.rem(rank + other, ranks)
            pl.semaphore_signal(barrier, inc=1, device_id=(shard, peer), device_id_type=MESH)
        wide_k[...] = k_ref[...].astype(F32).reshape(tokens * groups, width)
        wide_v[...] = v_ref[...].astype(F32).reshape(tokens * groups, width)
        for n in range(groups):
            rows = pl.ds(group_at(n, rank, ranks, share), tokens, stride=groups)
            own_k[n] = wide_k[rows].astype(BF16)
            own_v[n] = wide_v[rows].astype(BF16)
            if n == 0:
                pl.semaphore_wait(
                    barrier, ranks - 1 + has_next.astype(jnp.int32) + has_prev.astype(jnp.int32)
                )
                send_window(0)
        send_window(1)
        fill_bias(bias, lengths, shard * tokens, heads, chunk)
        for n in range(2, AHEAD):
            send_window(n)

    @pl.when(i + AHEAD < groups)
    def _():
        send_window(i + AHEAD)

    chunks, _, rows = bias.shape
    blocks = exponents.shape[0]

    def add_back(i):
        @pl.when(has_next)
        def _():
            back_copy(i).wait_recv()
            own[i] += back_in[i].astype(F32)

    def pass_on(i):
        add_back(i)
        cross_out[i] = own[i].astype(BF16)
        cross_copy(i).start()

    def finish(i):
        add_back(i)
        local = i - foreign
        total = own[i]
        for other in range(ranks - 1):
            cross_copy(other * share + local).wait_recv()
            total = total + cross_in[other * share + local].astype(F32)
        out_k[pl.ds(local, tokens, stride=share)] = total[0]
        out_v[pl.ds(local, tokens, stride=share)] = total[1]

    @pl.when(has_prev)
    def _():
        for copy in window_copies(i):
            copy.wait_recv()
        window_k[:tokens] = prev_k[i]
        window_v[:tokens] = prev_v[i]

    @pl.when(jnp.logical_not(has_prev))
    def _():
        window_k[:tokens] = jnp.zeros((tokens, width), BF16)
        window_v[:tokens] = jnp.zeros((tokens, width), BF16)

    window_k[tokens:] = own_k[i]
    window_v[tokens:] = own_v[i]
    factors = [
        row_factor(exponents, (j * blocks) // chunks, group, heads, rows) for j in range(chunks)
    ]
    out = group_terms(
        q_ref[...].reshape(tokens * heads, width), go_ref[...].reshape(tokens * heads, width),
        window_k, window_v, bias, factors, acc_k, acc_v,
    )
    gq_ref[:, pl.ds(group, 1)] = out.reshape(tokens, 1, heads, width)
    own[i, 0] = acc_k[tokens:]
    own[i, 1] = acc_v[tokens:] * unscale

    @pl.when(has_prev)
    def _():
        back_out[i, 0] = acc_k[:tokens].astype(BF16)
        back_out[i, 1] = (acc_v[:tokens] * unscale).astype(BF16)
        back_copy(i).start()

    @pl.when(jnp.logical_and(i >= LAG, i < foreign + LAG))
    def _():
        pass_on(i - LAG)

    @pl.when(i >= foreign + LAG)
    def _():
        finish(i - LAG)

    @pl.when(i == groups - 1)
    def _():
        for n in range(groups - LAG, groups):
            finish(n)
        gk_ref[...] = out_k[...].astype(BF16).reshape(tokens, share, width)
        gv_ref[...] = out_v[...].astype(BF16).reshape(tokens, share, width)

        @pl.when(has_next)
        def _():
            for n in range(groups):
                for copy in window_copies(n):
                    copy.wait_send()

        @pl.when(has_prev)
        def _():
            for n in range(groups):
                back_copy(n).wait_send()

        for n in range(foreign):
            cross_copy(n).wait_send()


def per_device(shards, ranks, queries, keys, values, grad_out, exponents, lengths):
    tokens, groups, heads, width = queries.shape
    chunks = 4
    chunk = tokens // chunks
    share = groups // ranks
    foreign = groups - share
    levels = jnp.swapaxes(exponents, 1, 2)
    smem = pl.BlockSpec(memory_space=pltpu.SMEM)
    vmem = pl.BlockSpec(memory_space=pltpu.VMEM)
    rows_spec = pl.BlockSpec(
        (tokens, 1, heads, width),
        lambda i: (0, group_at(i, lax.axis_index("tp"), ranks, share), 0, 0),
    )
    pair = (2, tokens, width)
    dma = pltpu.SemaphoreType.DMA
    return pl.pallas_call(
        functools.partial(fused_kernel, chunk, shards, ranks),
        grid=(groups,),
        in_specs=[smem, smem, rows_spec, rows_spec, vmem, vmem],
        out_specs=[vmem] * 3,
        out_shape=[
            pltpu.VMEM(queries.shape, BF16),
            pltpu.VMEM((tokens, share, width), BF16),
            pltpu.VMEM((tokens, share, width), BF16),
        ],
        scratch_shapes=[
            pltpu.VMEM((tokens * groups, width), F32),
            pltpu.VMEM((tokens * groups, width), F32),
            pltpu.VMEM((groups, tokens, width), BF16),
            pltpu.VMEM((groups, tokens, width), BF16),
            pltpu.VMEM((groups, tokens, width), BF16),
            pltpu.VMEM((groups, tokens, width), BF16),
            pltpu.VMEM((2 * tokens, width), BF16),
            pltpu.VMEM((2 * tokens, width), BF16),
            pltpu.VMEM((chunks, tokens + chunk, chunk * heads), F32),
            pltpu.VMEM((2 * tokens, width), F32),
            pltpu.VMEM((2 * tokens, width), F32),
            pltpu.VMEM((groups,) + pair, F32),
            pltpu.VMEM((groups,) + pair, BF16),
            pltpu.VMEM((groups,) + pair, BF16),
            pltpu.VMEM((foreign,) + pair, BF16),
            pltpu.VMEM((foreign,) + pair, BF16),
            pltpu.VMEM((tokens * share, width), F32),
            pltpu.VMEM((tokens * share, width), F32),
            dma((2, groups)), dma((2, groups)), dma((groups,)), dma((groups,)),
            dma((foreign,)), dma((foreign,)),
        ],
        compiler_params=pltpu.CompilerParams(
            collective_id=0, has_side_effects=True, vmem_limit_bytes=60 * 1024 * 1024
        ),
    )(lengths, levels, queries, grad_out, keys, values)


def solution(mesh):
    placed = (
        P("seq", None, "tp", None),
        P("seq", None, None),
        P("seq", None, None),
        P("seq", None, "tp", None),
        P("seq", None, "tp"),
        P(),
    )
    return jax.shard_map(
        functools.partial(per_device, mesh.shape["seq"], mesh.shape["tp"]),
        mesh=mesh,
        in_specs=placed,
        out_specs=(P("seq", None, "tp", None), P("seq", "tp", None), P("seq", "tp", None)),
        check_vma=False,
    )
```

```python
import functools
import math
import jax
import jax.numpy as jnp
from jax import lax
from jax.experimental import pallas as pl
from jax.experimental.pallas import tpu as pltpu
from jax.sharding import PartitionSpec as P

F32 = jnp.float32
BF16 = jnp.bfloat16
NT = (((1,), (1,)), ((), ()))
TN = (((0,), (0,)), ((), ()))
MESH = pl.DeviceIdType.MESH
AHEAD = 3
LAG = 2


def fill_bias(bias, lengths, first, heads, chunk):
    chunks, keys, rows = bias.shape
    for j in range(chunks):
        query_pos = first + chunk * j + lax.broadcasted_iota(jnp.int32, (1, rows), 1) // heads

        def step(d, carry):
            end, start = carry
            end = end + lengths[d]
            return end, jnp.where(query_pos >= end, end, start)

        _, start = lax.fori_loop(
            0, lengths.shape[0], step, (jnp.int32(0), jnp.zeros((1, rows), jnp.int32))
        )
        key_pos = first + chunk * (j + 1) - keys + lax.broadcasted_iota(jnp.int32, (keys, rows), 0)
        allowed = (key_pos >= start) & (key_pos <= query_pos)
        bias[j] = jnp.where(allowed, 0.0, -1e30).astype(F32)


def row_factor(exponents, block, group, heads, rows):
    head = lax.broadcasted_iota(jnp.int32, (1, rows), 1) % heads
    level = jnp.full((1, rows), exponents[block, 0, group], jnp.int32)
    for r in range(1, heads):
        level = jnp.where(head == r, exponents[block, r, group], level)
    factor = jnp.full((1, rows), 1.0, F32)
    for value in (-2, -1, 1, 2):
        factor = jnp.where(level == value, 2.0**value, factor)
    return factor


def group_terms(query, grad, key_ref, value_ref, bias, factors, grad_key, grad_value):
    chunks, keys, rows = bias.shape
    chunk = (key_ref.shape[0] - keys) // (chunks - 1)
    scaling = query.shape[1] ** -0.5
    grad_key[...] = jnp.zeros_like(grad_key)
    grad_value[...] = jnp.zeros_like(grad_value)
    grad_query = []

    def operands(j):
        window = pl.ds(chunk * j, keys)
        mine = slice(rows * j, rows * (j + 1))
        return window, query[mine], grad[mine], key_ref[window], value_ref[window]

    def products(j):
        _, q, g, k, v = operands(j)
        scores = lax.dot_general(k, q, NT, preferred_element_type=F32) + bias[j]
        return scores, lax.dot_general(v, g, NT, preferred_element_type=F32)

    def weights(j, scores, grad_probs):
        top = jnp.max(scores, axis=0, keepdims=True)
        e = jnp.exp2((scores - top) * (scaling * math.log2(math.e)))
        inverse = 1.0 / jnp.sum(e, axis=0, keepdims=True)
        delta = jnp.sum(e * grad_probs, axis=0, keepdims=True) * inverse
        p = e * (inverse * factors[j] * scaling)
        return p.astype(BF16), (p * (grad_probs - delta)).astype(BF16)

    def gradients(j, low, ds):
        window, q, g, k, _ = operands(j)
        grad_query.append(lax.dot_general(ds, k, TN, preferred_element_type=F32).astype(BF16))
        grad_key[window] += jnp.dot(ds, q, preferred_element_type=F32)
        grad_value[window] += jnp.dot(low, g, preferred_element_type=F32)

    first, second = {}, {}
    for t in range(chunks + 2):
        if t < chunks:
            first[t] = products(t)
        if 0 <= t - 2:
            gradients(t - 2, *second.pop(t - 2))
        if 0 <= t - 1 < chunks:
            second[t - 1] = weights(t - 1, *first.pop(t - 1))
    return jnp.concatenate(grad_query, axis=0)


def group_at(i, rank, ranks, share):
    return lax.rem(rank + 1 + i // share, ranks) * share + lax.rem(i, share)


def fused_kernel(
    chunk, shards, ranks,
    lengths, exponents, q_ref, go_ref, k_ref, v_ref,
    gq_ref, gk_ref, gv_ref,
    wide_k, wide_v, own_k, own_v, prev_k, prev_v, window_k, window_v, bias,
    acc_k, acc_v, own, back_out, back_in, cross_out, cross_in, out_k, out_v,
    win_send, win_recv, back_send, back_recv, cross_send, cross_recv,
):
    tokens, groups, width = k_ref.shape
    heads = q_ref.shape[2]
    share = groups // ranks
    foreign = groups - share
    shard, rank = lax.axis_index("seq"), lax.axis_index("tp")
    has_next, has_prev = shard < shards - 1, shard > 0
    unscale = width**0.5
    i = pl.program_id(0)
    group = group_at(i, rank, ranks, share)

    def window_copies(i):
        return [
            pltpu.make_async_remote_copy(
                src_ref=src.at[i], dst_ref=dst.at[i],
                send_sem=win_send.at[part, i], recv_sem=win_recv.at[part, i],
                device_id=(shard + 1, rank), device_id_type=MESH,
            )
            for part, (src, dst) in enumerate(((own_k, prev_k), (own_v, prev_v)))
        ]

    def send_window(i):
        @pl.when(has_next)
        def _():
            for copy in window_copies(i):
                copy.start()

    def back_copy(i):
        return pltpu.make_async_remote_copy(
            src_ref=back_out.at[i], dst_ref=back_in.at[i],
            send_sem=back_send.at[i], recv_sem=back_recv.at[i],
            device_id=(shard - 1, rank), device_id_type=MESH,
        )

    def cross_copy(i):
        return pltpu.make_async_remote_copy(
            src_ref=cross_out.at[i], dst_ref=cross_in.at[i],
            send_sem=cross_send.at[i], recv_sem=cross_recv.at[i],
            device_id=(shard, lax.rem(rank + 1 + i // share, ranks)), device_id_type=MESH,
        )

    @pl.when(i == 0)
    def _():
        barrier = pltpu.get_barrier_semaphore()

        @pl.when(has_next)
        def _():
            pl.semaphore_signal(barrier, inc=1, device_id=(shard + 1, rank), device_id_type=MESH)

        @pl.when(has_prev)
        def _():
            pl.semaphore_signal(barrier, inc=1, device_id=(shard - 1, rank), device_id_type=MESH)

        for other in range(1, ranks):
            peer = lax.rem(rank + other, ranks)
            pl.semaphore_signal(barrier, inc=1, device_id=(shard, peer), device_id_type=MESH)
        wide_k[...] = k_ref[...].astype(F32).reshape(tokens * groups, width)
        wide_v[...] = v_ref[...].astype(F32).reshape(tokens * groups, width)
        for n in range(groups):
            rows = pl.ds(group_at(n, rank, ranks, share), tokens, stride=groups)
            own_k[n] = wide_k[rows].astype(BF16)
            own_v[n] = wide_v[rows].astype(BF16)
            if n == 0:
                pl.semaphore_wait(
                    barrier, ranks - 1 + has_next.astype(jnp.int32) + has_prev.astype(jnp.int32)
                )
                send_window(0)
        send_window(1)
        fill_bias(bias, lengths, shard * tokens, heads, chunk)
        for n in range(2, AHEAD):
            send_window(n)

    @pl.when(i + AHEAD < groups)
    def _():
        send_window(i + AHEAD)

    chunks, _, rows = bias.shape
    blocks = exponents.shape[0]

    def add_back(i):
        @pl.when(has_next)
        def _():
            back_copy(i).wait_recv()
            own[i] += back_in[i].astype(F32)

    def pass_on(i):
        add_back(i)
        cross_out[i] = own[i].astype(BF16)
        cross_copy(i).start()

    def finish(i):
        add_back(i)
        local = i - foreign
        total = own[i]
        for other in range(ranks - 1):
            cross_copy(other * share + local).wait_recv()
            total = total + cross_in[other * share + local].astype(F32)
        out_k[pl.ds(local, tokens, stride=share)] = total[0]
        out_v[pl.ds(local, tokens, stride=share)] = total[1]

    @pl.when(has_prev)
    def _():
        for copy in window_copies(i):
            copy.wait_recv()
        window_k[:tokens] = prev_k[i]
        window_v[:tokens] = prev_v[i]

    @pl.when(jnp.logical_not(has_prev))
    def _():
        window_k[:tokens] = jnp.zeros((tokens, width), BF16)
        window_v[:tokens] = jnp.zeros((tokens, width), BF16)

    window_k[tokens:] = own_k[i]
    window_v[tokens:] = own_v[i]
    factors = [
        row_factor(exponents, (j * blocks) // chunks, group, heads, rows) for j in range(chunks)
    ]
    out = group_terms(
        q_ref[...].reshape(tokens * heads, width), go_ref[...].reshape(tokens * heads, width),
        window_k, window_v, bias, factors, acc_k, acc_v,
    )
    gq_ref[:, pl.ds(group, 1)] = out.reshape(tokens, 1, heads, width)
    own[i, 0] = acc_k[tokens:]
    own[i, 1] = acc_v[tokens:] * unscale

    @pl.when(has_prev)
    def _():
        back_out[i, 0] = acc_k[:tokens].astype(BF16)
        back_out[i, 1] = (acc_v[:tokens] * unscale).astype(BF16)
        back_copy(i).start()

    @pl.when(jnp.logical_and(i >= LAG, i < foreign + LAG))
    def _():
        pass_on(i - LAG)

    @pl.when(i >= foreign + LAG)
    def _():
        finish(i - LAG)

    @pl.when(i == groups - 1)
    def _():
        for n in range(groups - LAG, groups):
            finish(n)
        gk_ref[...] = out_k[...].astype(BF16).reshape(tokens, share, width)
        gv_ref[...] = out_v[...].astype(BF16).reshape(tokens, share, width)

        @pl.when(has_next)
        def _():
            for n in range(groups):
                for copy in window_copies(n):
                    copy.wait_send()

        @pl.when(has_prev)
        def _():
            for n in range(groups):
                back_copy(n).wait_send()

        for n in range(foreign):
            cross_copy(n).wait_send()


def write_kernel(gq, gk, gv, gq_hbm, gk_hbm, gv_hbm, sems):
    copies = [
        pltpu.make_async_copy(src, dst, sems.at[n])
        for n, (src, dst) in enumerate(((gq, gq_hbm), (gk, gk_hbm), (gv, gv_hbm)))
    ]
    for copy in copies:
        copy.start()
    for copy in copies:
        copy.wait()


def per_device(shards, ranks, queries, keys, values, grad_out, exponents, lengths):
    tokens, groups, heads, width = queries.shape
    chunks = 4
    chunk = tokens // chunks
    share = groups // ranks
    foreign = groups - share
    levels = jnp.swapaxes(exponents, 1, 2)
    smem = pl.BlockSpec(memory_space=pltpu.SMEM)
    vmem = pl.BlockSpec(memory_space=pltpu.VMEM)
    rows_spec = pl.BlockSpec(
        (tokens, 1, heads, width),
        lambda i: (0, group_at(i, lax.axis_index("tp"), ranks, share), 0, 0),
    )
    pair = (2, tokens, width)
    dma = pltpu.SemaphoreType.DMA
    results = pl.pallas_call(
        functools.partial(fused_kernel, chunk, shards, ranks),
        grid=(groups,),
        in_specs=[smem, smem, rows_spec, rows_spec, vmem, vmem],
        out_specs=[vmem] * 3,
        out_shape=[
            pltpu.VMEM(queries.shape, BF16),
            pltpu.VMEM((tokens, share, width), BF16),
            pltpu.VMEM((tokens, share, width), BF16),
        ],
        scratch_shapes=[
            pltpu.VMEM((tokens * groups, width), F32),
            pltpu.VMEM((tokens * groups, width), F32),
            pltpu.VMEM((groups, tokens, width), BF16),
            pltpu.VMEM((groups, tokens, width), BF16),
            pltpu.VMEM((groups, tokens, width), BF16),
            pltpu.VMEM((groups, tokens, width), BF16),
            pltpu.VMEM((2 * tokens, width), BF16),
            pltpu.VMEM((2 * tokens, width), BF16),
            pltpu.VMEM((chunks, tokens + chunk, chunk * heads), F32),
            pltpu.VMEM((2 * tokens, width), F32),
            pltpu.VMEM((2 * tokens, width), F32),
            pltpu.VMEM((groups,) + pair, F32),
            pltpu.VMEM((groups,) + pair, BF16),
            pltpu.VMEM((groups,) + pair, BF16),
            pltpu.VMEM((foreign,) + pair, BF16),
            pltpu.VMEM((foreign,) + pair, BF16),
            pltpu.VMEM((tokens * share, width), F32),
            pltpu.VMEM((tokens * share, width), F32),
            dma((2, groups)), dma((2, groups)), dma((groups,)), dma((groups,)),
            dma((foreign,)), dma((foreign,)),
        ],
        compiler_params=pltpu.CompilerParams(
            collective_id=0, has_side_effects=True, vmem_limit_bytes=60 * 1024 * 1024
        ),
    )(lengths, levels, queries, grad_out, keys, values)
    return pl.pallas_call(
        write_kernel,
        in_specs=[vmem] * 3,
        out_specs=[pl.BlockSpec(memory_space=pltpu.HBM)] * 3,
        out_shape=[jax.ShapeDtypeStruct(r.shape, r.dtype) for r in results],
        scratch_shapes=[dma((3,))],
    )(*results)


def solution(mesh):
    placed = (
        P("seq", None, "tp", None),
        P("seq", None, None),
        P("seq", None, None),
        P("seq", None, "tp", None),
        P("seq", None, "tp"),
        P(),
    )
    return jax.shard_map(
        functools.partial(per_device, mesh.shape["seq"], mesh.shape["tp"]),
        mesh=mesh,
        in_specs=placed,
        out_specs=(P("seq", None, "tp", None), P("seq", "tp", None), P("seq", "tp", None)),
        check_vma=False,
    )
```

```python
import functools
import math
import jax
import jax.numpy as jnp
from jax import lax
from jax.experimental import pallas as pl
from jax.experimental.pallas import tpu as pltpu
from jax.sharding import PartitionSpec as P

F32 = jnp.float32
BF16 = jnp.bfloat16
NT = (((1,), (1,)), ((), ()))
TN = (((0,), (0,)), ((), ()))
MESH = pl.DeviceIdType.MESH
AHEAD = 2
LAG = 3


def fill_bias(bias, lengths, first, heads, chunk):
    chunks, keys, rows = bias.shape
    for j in range(chunks):
        query_pos = first + chunk * j + lax.broadcasted_iota(jnp.int32, (1, rows), 1) // heads

        def step(d, carry):
            end, start = carry
            end = end + lengths[d]
            return end, jnp.where(query_pos >= end, end, start)

        _, start = lax.fori_loop(
            0, lengths.shape[0], step, (jnp.int32(0), jnp.zeros((1, rows), jnp.int32))
        )
        key_pos = first + chunk * (j + 1) - keys + lax.broadcasted_iota(jnp.int32, (keys, rows), 0)
        allowed = (key_pos >= start) & (key_pos <= query_pos)
        bias[j] = jnp.where(allowed, 0.0, -1e30).astype(F32)


def row_factor(exponents, block, group, heads, rows):
    head = lax.broadcasted_iota(jnp.int32, (1, rows), 1) % heads
    level = jnp.full((1, rows), exponents[block, 0, group], jnp.int32)
    for r in range(1, heads):
        level = jnp.where(head == r, exponents[block, r, group], level)
    factor = jnp.full((1, rows), 1.0, F32)
    for value in (-2, -1, 1, 2):
        factor = jnp.where(level == value, 2.0**value, factor)
    return factor


def group_terms(query, grad, key_ref, value_ref, bias, factors, grad_key, grad_value):
    chunks, keys, rows = bias.shape
    chunk = (key_ref.shape[0] - keys) // (chunks - 1)
    scaling = query.shape[1] ** -0.5
    grad_key[...] = jnp.zeros_like(grad_key)
    grad_value[...] = jnp.zeros_like(grad_value)
    grad_query = []

    def operands(j):
        window = pl.ds(chunk * j, keys)
        mine = slice(rows * j, rows * (j + 1))
        return window, query[mine], grad[mine], key_ref[window], value_ref[window]

    def products(j):
        _, q, g, k, v = operands(j)
        scores = lax.dot_general(k, q, NT, preferred_element_type=F32) + bias[j]
        return scores, lax.dot_general(v, g, NT, preferred_element_type=F32)

    def weights(j, scores, grad_probs):
        top = jnp.max(scores, axis=0, keepdims=True)
        e = jnp.exp2((scores - top) * (scaling * math.log2(math.e)))
        inverse = 1.0 / jnp.sum(e, axis=0, keepdims=True)
        delta = jnp.sum(e * grad_probs, axis=0, keepdims=True) * inverse
        p = e * (inverse * factors[j] * scaling)
        return p.astype(BF16), (p * (grad_probs - delta)).astype(BF16)

    def gradients(j, low, ds):
        window, q, g, k, _ = operands(j)
        grad_query.append(lax.dot_general(ds, k, TN, preferred_element_type=F32).astype(BF16))
        grad_key[window] += jnp.dot(ds, q, preferred_element_type=F32)
        grad_value[window] += jnp.dot(low, g, preferred_element_type=F32)

    first, second = {}, {}
    for t in range(chunks + 2):
        if t < chunks:
            first[t] = products(t)
        if 0 <= t - 2:
            gradients(t - 2, *second.pop(t - 2))
        if 0 <= t - 1 < chunks:
            second[t - 1] = weights(t - 1, *first.pop(t - 1))
    return jnp.concatenate(grad_query, axis=0)


def group_at(i, rank, ranks, share):
    return lax.rem(rank + 1 + i // share, ranks) * share + lax.rem(i, share)


def fused_kernel(
    chunk, shards, ranks,
    lengths, exponents, q_ref, go_ref, k_ref, v_ref,
    gq_ref, gk_ref, gv_ref,
    wide_k, wide_v, own_k, own_v, prev_k, prev_v, window_k, window_v, bias,
    acc_k, acc_v, own, back_out, back_in, cross_out, cross_in, out_k, out_v,
    win_send, win_recv, back_send, back_recv, cross_send, cross_recv,
):
    tokens, groups, width = k_ref.shape
    heads = q_ref.shape[2]
    share = groups // ranks
    foreign = groups - share
    shard, rank = lax.axis_index("seq"), lax.axis_index("tp")
    has_next, has_prev = shard < shards - 1, shard > 0
    unscale = width**0.5
    i = pl.program_id(0)
    group = group_at(i, rank, ranks, share)

    def window_copies(i):
        return [
            pltpu.make_async_remote_copy(
                src_ref=src.at[i], dst_ref=dst.at[i],
                send_sem=win_send.at[part, i], recv_sem=win_recv.at[part, i],
                device_id=(shard + 1, rank), device_id_type=MESH,
            )
            for part, (src, dst) in enumerate(((own_k, prev_k), (own_v, prev_v)))
        ]

    def send_window(i):
        @pl.when(has_next)
        def _():
            for copy in window_copies(i):
                copy.start()

    def back_copy(i):
        return pltpu.make_async_remote_copy(
            src_ref=back_out.at[i], dst_ref=back_in.at[i],
            send_sem=back_send.at[i], recv_sem=back_recv.at[i],
            device_id=(shard - 1, rank), device_id_type=MESH,
        )

    def cross_copy(i):
        return pltpu.make_async_remote_copy(
            src_ref=cross_out.at[i], dst_ref=cross_in.at[i],
            send_sem=cross_send.at[i], recv_sem=cross_recv.at[i],
            device_id=(shard, lax.rem(rank + 1 + i // share, ranks)), device_id_type=MESH,
        )

    @pl.when(i == 0)
    def _():
        barrier = pltpu.get_barrier_semaphore()

        @pl.when(has_next)
        def _():
            pl.semaphore_signal(barrier, inc=1, device_id=(shard + 1, rank), device_id_type=MESH)

        @pl.when(has_prev)
        def _():
            pl.semaphore_signal(barrier, inc=1, device_id=(shard - 1, rank), device_id_type=MESH)

        for other in range(1, ranks):
            peer = lax.rem(rank + other, ranks)
            pl.semaphore_signal(barrier, inc=1, device_id=(shard, peer), device_id_type=MESH)
        wide_k[...] = k_ref[...].astype(F32).reshape(tokens * groups, width)
        wide_v[...] = v_ref[...].astype(F32).reshape(tokens * groups, width)
        for n in range(groups):
            rows = pl.ds(group_at(n, rank, ranks, share), tokens, stride=groups)
            own_k[n] = wide_k[rows].astype(BF16)
            own_v[n] = wide_v[rows].astype(BF16)
            if n == 0:
                pl.semaphore_wait(
                    barrier, ranks - 1 + has_next.astype(jnp.int32) + has_prev.astype(jnp.int32)
                )
                send_window(0)
        fill_bias(bias, lengths, shard * tokens, heads, chunk)
        for n in range(1, AHEAD):
            send_window(n)

    @pl.when(i + AHEAD < groups)
    def _():
        send_window(i + AHEAD)

    chunks, _, rows = bias.shape
    blocks = exponents.shape[0]

    def add_back(i):
        @pl.when(has_next)
        def _():
            back_copy(i).wait_recv()
            own[i] += back_in[i].astype(F32)

    def pass_on(i):
        add_back(i)
        cross_out[i] = own[i].astype(BF16)
        cross_copy(i).start()

    def finish(i):
        add_back(i)
        local = i - foreign
        total = own[i]
        for other in range(ranks - 1):
            cross_copy(other * share + local).wait_recv()
            total = total + cross_in[other * share + local].astype(F32)
        out_k[pl.ds(local, tokens, stride=share)] = total[0]
        out_v[pl.ds(local, tokens, stride=share)] = total[1]

    @pl.when(has_prev)
    def _():
        for copy in window_copies(i):
            copy.wait_recv()
        window_k[:tokens] = prev_k[i]
        window_v[:tokens] = prev_v[i]

    @pl.when(jnp.logical_not(has_prev))
    def _():
        window_k[:tokens] = jnp.zeros((tokens, width), BF16)
        window_v[:tokens] = jnp.zeros((tokens, width), BF16)

    window_k[tokens:] = own_k[i]
    window_v[tokens:] = own_v[i]
    factors = [
        row_factor(exponents, (j * blocks) // chunks, group, heads, rows) for j in range(chunks)
    ]
    out = group_terms(
        q_ref[...].reshape(tokens * heads, width), go_ref[...].reshape(tokens * heads, width),
        window_k, window_v, bias, factors, acc_k, acc_v,
    )
    gq_ref[:, pl.ds(group, 1)] = out.reshape(tokens, 1, heads, width)
    own[i, 0] = acc_k[tokens:]
    own[i, 1] = acc_v[tokens:] * unscale

    @pl.when(has_prev)
    def _():
        back_out[i, 0] = acc_k[:tokens].astype(BF16)
        back_out[i, 1] = (acc_v[:tokens] * unscale).astype(BF16)
        back_copy(i).start()

    @pl.when(jnp.logical_and(i >= LAG, i < foreign + LAG))
    def _():
        pass_on(i - LAG)

    @pl.when(i >= foreign + LAG)
    def _():
        finish(i - LAG)

    @pl.when(i == groups - 1)
    def _():
        for n in range(groups - LAG, groups):
            finish(n)
        gk_ref[...] = out_k[...].astype(BF16).reshape(tokens, share, width)
        gv_ref[...] = out_v[...].astype(BF16).reshape(tokens, share, width)

        @pl.when(has_next)
        def _():
            for n in range(groups):
                for copy in window_copies(n):
                    copy.wait_send()

        @pl.when(has_prev)
        def _():
            for n in range(groups):
                back_copy(n).wait_send()

        for n in range(foreign):
            cross_copy(n).wait_send()


def per_device(shards, ranks, queries, keys, values, grad_out, exponents, lengths):
    tokens, groups, heads, width = queries.shape
    chunks = 4
    chunk = tokens // chunks
    share = groups // ranks
    foreign = groups - share
    levels = jnp.swapaxes(exponents, 1, 2)
    smem = pl.BlockSpec(memory_space=pltpu.SMEM)
    vmem = pl.BlockSpec(memory_space=pltpu.VMEM)
    rows_spec = pl.BlockSpec(
        (tokens, 1, heads, width),
        lambda i: (0, group_at(i, lax.axis_index("tp"), ranks, share), 0, 0),
    )
    pair = (2, tokens, width)
    dma = pltpu.SemaphoreType.DMA
    return pl.pallas_call(
        functools.partial(fused_kernel, chunk, shards, ranks),
        grid=(groups,),
        in_specs=[smem, smem, rows_spec, rows_spec, vmem, vmem],
        out_specs=[vmem] * 3,
        out_shape=[
            pltpu.VMEM(queries.shape, BF16),
            pltpu.VMEM((tokens, share, width), BF16),
            pltpu.VMEM((tokens, share, width), BF16),
        ],
        scratch_shapes=[
            pltpu.VMEM((tokens * groups, width), F32),
            pltpu.VMEM((tokens * groups, width), F32),
            pltpu.VMEM((groups, tokens, width), BF16),
            pltpu.VMEM((groups, tokens, width), BF16),
            pltpu.VMEM((groups, tokens, width), BF16),
            pltpu.VMEM((groups, tokens, width), BF16),
            pltpu.VMEM((2 * tokens, width), BF16),
            pltpu.VMEM((2 * tokens, width), BF16),
            pltpu.VMEM((chunks, tokens + chunk, chunk * heads), F32),
            pltpu.VMEM((2 * tokens, width), F32),
            pltpu.VMEM((2 * tokens, width), F32),
            pltpu.VMEM((groups,) + pair, F32),
            pltpu.VMEM((groups,) + pair, BF16),
            pltpu.VMEM((groups,) + pair, BF16),
            pltpu.VMEM((foreign,) + pair, BF16),
            pltpu.VMEM((foreign,) + pair, BF16),
            pltpu.VMEM((tokens * share, width), F32),
            pltpu.VMEM((tokens * share, width), F32),
            dma((2, groups)), dma((2, groups)), dma((groups,)), dma((groups,)),
            dma((foreign,)), dma((foreign,)),
        ],
        compiler_params=pltpu.CompilerParams(
            collective_id=0, has_side_effects=True, vmem_limit_bytes=60 * 1024 * 1024
        ),
    )(lengths, levels, queries, grad_out, keys, values)


def solution(mesh):
    placed = (
        P("seq", None, "tp", None),
        P("seq", None, None),
        P("seq", None, None),
        P("seq", None, "tp", None),
        P("seq", None, "tp"),
        P(),
    )
    return jax.shard_map(
        functools.partial(per_device, mesh.shape["seq"], mesh.shape["tp"]),
        mesh=mesh,
        in_specs=placed,
        out_specs=(P("seq", None, "tp", None), P("seq", "tp", None), P("seq", "tp", None)),
        check_vma=False,
    )
```

```python
import functools
import math
import jax
import jax.numpy as jnp
from jax import lax
from jax.experimental import pallas as pl
from jax.experimental.pallas import tpu as pltpu
from jax.sharding import PartitionSpec as P

F32 = jnp.float32
BF16 = jnp.bfloat16
NT = (((1,), (1,)), ((), ()))
TN = (((0,), (0,)), ((), ()))
MESH = pl.DeviceIdType.MESH
AHEAD = 4
LAG = 3


def fill_bias(bias, lengths, first, heads, chunk):
    chunks, keys, rows = bias.shape
    for j in range(chunks):
        query_pos = first + chunk * j + lax.broadcasted_iota(jnp.int32, (1, rows), 1) // heads

        def step(d, carry):
            end, start = carry
            end = end + lengths[d]
            return end, jnp.where(query_pos >= end, end, start)

        _, start = lax.fori_loop(
            0, lengths.shape[0], step, (jnp.int32(0), jnp.zeros((1, rows), jnp.int32))
        )
        key_pos = first + chunk * (j + 1) - keys + lax.broadcasted_iota(jnp.int32, (keys, rows), 0)
        allowed = (key_pos >= start) & (key_pos <= query_pos)
        bias[j] = jnp.where(allowed, 0.0, -1e30).astype(F32)


def row_factor(exponents, block, group, heads, rows):
    head = lax.broadcasted_iota(jnp.int32, (1, rows), 1) % heads
    level = jnp.full((1, rows), exponents[block, 0, group], jnp.int32)
    for r in range(1, heads):
        level = jnp.where(head == r, exponents[block, r, group], level)
    factor = jnp.full((1, rows), 1.0, F32)
    for value in (-2, -1, 1, 2):
        factor = jnp.where(level == value, 2.0**value, factor)
    return factor


def group_terms(query, grad, key_ref, value_ref, bias, factors, grad_key, grad_value):
    chunks, keys, rows = bias.shape
    chunk = (key_ref.shape[0] - keys) // (chunks - 1)
    scaling = query.shape[1] ** -0.5
    grad_key[...] = jnp.zeros_like(grad_key)
    grad_value[...] = jnp.zeros_like(grad_value)
    grad_query = []

    def operands(j):
        window = pl.ds(chunk * j, keys)
        mine = slice(rows * j, rows * (j + 1))
        return window, query[mine], grad[mine], key_ref[window], value_ref[window]

    def products(j):
        _, q, g, k, v = operands(j)
        scores = lax.dot_general(k, q, NT, preferred_element_type=F32) + bias[j]
        return scores, lax.dot_general(v, g, NT, preferred_element_type=F32)

    def weights(j, scores, grad_probs):
        top = jnp.max(scores, axis=0, keepdims=True)
        e = jnp.exp2((scores - top) * (scaling * math.log2(math.e)))
        inverse = 1.0 / jnp.sum(e, axis=0, keepdims=True)
        delta = jnp.sum(e * grad_probs, axis=0, keepdims=True) * inverse
        p = e * (inverse * factors[j] * scaling)
        return p.astype(BF16), (p * (grad_probs - delta)).astype(BF16)

    def gradients(j, low, ds):
        window, q, g, k, _ = operands(j)
        grad_query.append(lax.dot_general(ds, k, TN, preferred_element_type=F32).astype(BF16))
        grad_key[window] += jnp.dot(ds, q, preferred_element_type=F32)
        grad_value[window] += jnp.dot(low, g, preferred_element_type=F32)

    first, second = {}, {}
    for t in range(chunks + 2):
        if t < chunks:
            first[t] = products(t)
        if 0 <= t - 2:
            gradients(t - 2, *second.pop(t - 2))
        if 0 <= t - 1 < chunks:
            second[t - 1] = weights(t - 1, *first.pop(t - 1))
    return jnp.concatenate(grad_query, axis=0)


def group_at(i, rank, ranks, share):
    return lax.rem(rank + 1 + i // share, ranks) * share + lax.rem(i, share)


def fused_kernel(
    chunk, shards, ranks,
    lengths, exponents, q_ref, go_ref, k_ref, v_ref,
    gq_ref, gk_ref, gv_ref,
    wide_k, wide_v, own_k, own_v, prev_k, prev_v, window_k, window_v, bias,
    acc_k, acc_v, own, back_out, back_in, cross_out, cross_in, out_k, out_v,
    win_send, win_recv, back_send, back_recv, cross_send, cross_recv,
):
    tokens, groups, width = k_ref.shape
    heads = q_ref.shape[2]
    share = groups // ranks
    foreign = groups - share
    shard, rank = lax.axis_index("seq"), lax.axis_index("tp")
    has_next, has_prev = shard < shards - 1, shard > 0
    unscale = width**0.5
    i = pl.program_id(0)
    group = group_at(i, rank, ranks, share)

    def window_copies(i):
        return [
            pltpu.make_async_remote_copy(
                src_ref=src.at[i], dst_ref=dst.at[i],
                send_sem=win_send.at[part, i], recv_sem=win_recv.at[part, i],
                device_id=(shard + 1, rank), device_id_type=MESH,
            )
            for part, (src, dst) in enumerate(((own_k, prev_k), (own_v, prev_v)))
        ]

    def send_window(i):
        @pl.when(has_next)
        def _():
            for copy in window_copies(i):
                copy.start()

    def back_copy(i):
        return pltpu.make_async_remote_copy(
            src_ref=back_out.at[i], dst_ref=back_in.at[i],
            send_sem=back_send.at[i], recv_sem=back_recv.at[i],
            device_id=(shard - 1, rank), device_id_type=MESH,
        )

    def cross_copy(i):
        return pltpu.make_async_remote_copy(
            src_ref=cross_out.at[i], dst_ref=cross_in.at[i],
            send_sem=cross_send.at[i], recv_sem=cross_recv.at[i],
            device_id=(shard, lax.rem(rank + 1 + i // share, ranks)), device_id_type=MESH,
        )

    @pl.when(i == 0)
    def _():
        barrier = pltpu.get_barrier_semaphore()

        @pl.when(has_next)
        def _():
            pl.semaphore_signal(barrier, inc=1, device_id=(shard + 1, rank), device_id_type=MESH)

        @pl.when(has_prev)
        def _():
            pl.semaphore_signal(barrier, inc=1, device_id=(shard - 1, rank), device_id_type=MESH)

        for other in range(1, ranks):
            peer = lax.rem(rank + other, ranks)
            pl.semaphore_signal(barrier, inc=1, device_id=(shard, peer), device_id_type=MESH)
        wide_k[...] = k_ref[...].astype(F32).reshape(tokens * groups, width)
        wide_v[...] = v_ref[...].astype(F32).reshape(tokens * groups, width)
        for n in range(groups):
            rows = pl.ds(group_at(n, rank, ranks, share), tokens, stride=groups)
            own_k[n] = wide_k[rows].astype(BF16)
            own_v[n] = wide_v[rows].astype(BF16)
            if n == 0:
                pl.semaphore_wait(
                    barrier, ranks - 1 + has_next.astype(jnp.int32) + has_prev.astype(jnp.int32)
                )
                send_window(0)
        fill_bias(bias, lengths, shard * tokens, heads, chunk)
        for n in range(1, AHEAD):
            send_window(n)

    @pl.when(i + AHEAD < groups)
    def _():
        send_window(i + AHEAD)

    chunks, _, rows = bias.shape
    blocks = exponents.shape[0]

    def add_back(i):
        @pl.when(has_next)
        def _():
            back_copy(i).wait_recv()
            own[i] += back_in[i].astype(F32)

    def pass_on(i):
        add_back(i)
        cross_out[i] = own[i].astype(BF16)
        cross_copy(i).start()

    def finish(i):
        add_back(i)
        local = i - foreign
        total = own[i]
        for other in range(ranks - 1):
            cross_copy(other * share + local).wait_recv()
            total = total + cross_in[other * share + local].astype(F32)
        out_k[pl.ds(local, tokens, stride=share)] = total[0]
        out_v[pl.ds(local, tokens, stride=share)] = total[1]

    @pl.when(has_prev)
    def _():
        for copy in window_copies(i):
            copy.wait_recv()
        window_k[:tokens] = prev_k[i]
        window_v[:tokens] = prev_v[i]

    @pl.when(jnp.logical_not(has_prev))
    def _():
        window_k[:tokens] = jnp.zeros((tokens, width), BF16)
        window_v[:tokens] = jnp.zeros((tokens, width), BF16)

    window_k[tokens:] = own_k[i]
    window_v[tokens:] = own_v[i]
    factors = [
        row_factor(exponents, (j * blocks) // chunks, group, heads, rows) for j in range(chunks)
    ]
    out = group_terms(
        q_ref[...].reshape(tokens * heads, width), go_ref[...].reshape(tokens * heads, width),
        window_k, window_v, bias, factors, acc_k, acc_v,
    )
    gq_ref[:, pl.ds(group, 1)] = out.reshape(tokens, 1, heads, width)
    own[i, 0] = acc_k[tokens:]
    own[i, 1] = acc_v[tokens:] * unscale

    @pl.when(has_prev)
    def _():
        back_out[i, 0] = acc_k[:tokens].astype(BF16)
        back_out[i, 1] = (acc_v[:tokens] * unscale).astype(BF16)
        back_copy(i).start()

    @pl.when(jnp.logical_and(i >= LAG, i < foreign + LAG))
    def _():
        pass_on(i - LAG)

    @pl.when(i >= foreign + LAG)
    def _():
        finish(i - LAG)

    @pl.when(i == groups - 1)
    def _():
        for n in range(groups - LAG, groups):
            finish(n)
        gk_ref[...] = out_k[...].astype(BF16).reshape(tokens, share, width)
        gv_ref[...] = out_v[...].astype(BF16).reshape(tokens, share, width)

        @pl.when(has_next)
        def _():
            for n in range(groups):
                for copy in window_copies(n):
                    copy.wait_send()

        @pl.when(has_prev)
        def _():
            for n in range(groups):
                back_copy(n).wait_send()

        for n in range(foreign):
            cross_copy(n).wait_send()


def per_device(shards, ranks, queries, keys, values, grad_out, exponents, lengths):
    tokens, groups, heads, width = queries.shape
    chunks = 4
    chunk = tokens // chunks
    share = groups // ranks
    foreign = groups - share
    levels = jnp.swapaxes(exponents, 1, 2)
    smem = pl.BlockSpec(memory_space=pltpu.SMEM)
    vmem = pl.BlockSpec(memory_space=pltpu.VMEM)
    rows_spec = pl.BlockSpec(
        (tokens, 1, heads, width),
        lambda i: (0, group_at(i, lax.axis_index("tp"), ranks, share), 0, 0),
    )
    pair = (2, tokens, width)
    dma = pltpu.SemaphoreType.DMA
    return pl.pallas_call(
        functools.partial(fused_kernel, chunk, shards, ranks),
        grid=(groups,),
        in_specs=[smem, smem, rows_spec, rows_spec, vmem, vmem],
        out_specs=[vmem] * 3,
        out_shape=[
            pltpu.VMEM(queries.shape, BF16),
            pltpu.VMEM((tokens, share, width), BF16),
            pltpu.VMEM((tokens, share, width), BF16),
        ],
        scratch_shapes=[
            pltpu.VMEM((tokens * groups, width), F32),
            pltpu.VMEM((tokens * groups, width), F32),
            pltpu.VMEM((groups, tokens, width), BF16),
            pltpu.VMEM((groups, tokens, width), BF16),
            pltpu.VMEM((groups, tokens, width), BF16),
            pltpu.VMEM((groups, tokens, width), BF16),
            pltpu.VMEM((2 * tokens, width), BF16),
            pltpu.VMEM((2 * tokens, width), BF16),
            pltpu.VMEM((chunks, tokens + chunk, chunk * heads), F32),
            pltpu.VMEM((2 * tokens, width), F32),
            pltpu.VMEM((2 * tokens, width), F32),
            pltpu.VMEM((groups,) + pair, F32),
            pltpu.VMEM((groups,) + pair, BF16),
            pltpu.VMEM((groups,) + pair, BF16),
            pltpu.VMEM((foreign,) + pair, BF16),
            pltpu.VMEM((foreign,) + pair, BF16),
            pltpu.VMEM((tokens * share, width), F32),
            pltpu.VMEM((tokens * share, width), F32),
            dma((2, groups)), dma((2, groups)), dma((groups,)), dma((groups,)),
            dma((foreign,)), dma((foreign,)),
        ],
        compiler_params=pltpu.CompilerParams(
            collective_id=0, has_side_effects=True, vmem_limit_bytes=60 * 1024 * 1024
        ),
    )(lengths, levels, queries, grad_out, keys, values)


def solution(mesh):
    placed = (
        P("seq", None, "tp", None),
        P("seq", None, None),
        P("seq", None, None),
        P("seq", None, "tp", None),
        P("seq", None, "tp"),
        P(),
    )
    return jax.shard_map(
        functools.partial(per_device, mesh.shape["seq"], mesh.shape["tp"]),
        mesh=mesh,
        in_specs=placed,
        out_specs=(P("seq", None, "tp", None), P("seq", "tp", None), P("seq", "tp", None)),
        check_vma=False,
    )
```
